32 devices in a mesh: seq: 16 (over z, y, x), head: 2 (over core).
Axes of the slice: x: 2, y: 2, z: 4, core: 2. Of those that a mesh axis runs over, the one named last changes fastest.
Arguments:
- query: bfloat16 [2048, 4096], P('seq', 'head'), may hold values from -6 to 6
- keys: bfloat16 [2048, 2, 4096], P('seq', None, 'head'), may hold values from -8 to 8
- values: bfloat16 [2048, 2, 4096], P('seq', None, 'head'), may hold values from -6 to 6
- beta: float32 [2, 32, 2048], P(None, 'head', 'seq'), may hold values from 0.001 to 1
- gate_log: float32 [32, 2048], P('head', 'seq'), may hold values from -0.7 to 0
- house_count: int32 [2048], P('seq'), may hold values from 1 to 2
- out_gate: bfloat16 [2048, 4096], P('seq', 'head'), may hold values from -6 to 6
- norm_gain: float32 [128], replicated, may hold values from 0.1 to 1.9
- out_weight: bfloat16 [4096, 4096], P(None, 'head'), may hold values from -0.09375 to 0.09375
Outputs:
- mixed: bfloat16 [2048, 4096], P('seq', 'head')
The draws below stay inside these ranges and needn't reach their ends.
All inputs are finite; a program needn't handle non-finite values.
Results may differ from the reference program's by a relative error of at most 0.0049.
Values may be sent and summed in bfloat16 or wider, within the bound.
A program may use at most 320 MiB of HBM per device.

```python
import math
import jax
import jax.numpy as jnp
from jax import lax

H = 32
DK = 128
DV = 128
D = 4096
NH = 2
DOCUMENT_TOKENS = 2048


def head_kinds(key):
    order = jax.random.permutation(jax.random.fold_in(key, 7), H)
    fast_count = H // 2
    return (order < fast_count)[:, None]


def draw_gate_log(key, part):
    fast_key, slow_key, rough_key, position_key, retained_key = jax.random.split(jax.random.fold_in(key, 3), 5)
    is_fast = head_kinds(key)
    rate_fast = math.log(10.0) / jax.random.uniform(fast_key, (H, 1), minval=30.0, maxval=50.0)
    rate_slow = jax.random.uniform(slow_key, (H, 1), minval=0.1, maxval=0.4) / DOCUMENT_TOKENS
    head_decay_rates = jnp.where(is_fast, rate_fast, rate_slow)
    noise_level = jnp.exp(jax.random.uniform(rough_key, (H, DOCUMENT_TOKENS), minval=-math.log(2.0), maxval=math.log(2.0)))
    cluster_positions = jax.random.randint(position_key, (3, 1), 0, DOCUMENT_TOKENS)
    cluster_keep_flags = jax.random.uniform(retained_key, (3, 1), minval=0.6, maxval=0.8)
    token_positions = jnp.arange(DOCUMENT_TOKENS, dtype=jnp.int32)[None, :]
    token_clusters = jnp.sum(jnp.where(token_positions == cluster_positions, jnp.log(cluster_keep_flags), 0.0), axis=0)
    return (-head_decay_rates * noise_level + token_clusters[None, :]).astype(jnp.float32)


def draw_beta(key, part):
    fast_key, slow_key = jax.random.split(jax.random.fold_in(key, 5), 2)
    is_fast = head_kinds(key)
    fast_values = jnp.exp(jax.random.uniform(fast_key, (NH, H, DOCUMENT_TOKENS), minval=math.log(0.05), maxval=0.0))
    slow_values = jnp.exp(jax.random.uniform(slow_key, (NH, H, DOCUMENT_TOKENS), minval=math.log(0.001), maxval=math.log(0.01)))
    return jnp.where(is_fast[None, :, :], fast_values, slow_values).astype(jnp.float32)


def draw_keys(key, part):
    noise_key, shared_key, mix_key = jax.random.split(jax.random.fold_in(key, 11), 3)
    shared = jax.random.normal(shared_key, (1, 1, H, DK), jnp.float32)
    mixing = jax.random.uniform(mix_key, (1, 1, H, 1), minval=0.5, maxval=1.0)
    noise = jax.random.normal(noise_key, (DOCUMENT_TOKENS, NH, H, DK), jnp.float32)
    combined = jnp.clip(noise + mixing * shared, -8.0, 8.0)
    return combined.reshape(DOCUMENT_TOKENS, NH, H * DK).astype(jnp.bfloat16)


def touch_ends(array, stream_key, smallest, high):
    dims = array.shape
    place = [jax.random.randint(jax.random.fold_in(stream_key, axis), (), 0, dims[axis]) for axis in range(len(dims))]
    array = array.at[tuple(place)].set(smallest)
    longest = dims.index(max(dims))
    place[longest] = (place[longest] + 1) % dims[longest]
    return array.at[tuple(place)].set(high)


def block_levels(rng, shape, cuts, least, high):
    loudness, own = 1.0, jax.random.fold_in(rng, 6)
    for axis_at, blocks in cuts:
        draws = jnp.exp(jax.random.uniform(jax.random.fold_in(own, axis_at), (blocks,), jnp.float32, least / len(cuts), high / len(cuts)))
        loudness = loudness * jnp.repeat(draws, shape[axis_at] // blocks).reshape([-1 if axis == axis_at else 1 for axis in range(len(shape))])
    return loudness


def bell_draw(key, shape, scale, reach, cuts=(), kind=jnp.bfloat16):
    array = scale * jax.random.normal(key, shape, jnp.float32)
    if cuts:
        array = array * block_levels(key, shape, cuts, -0.22, 0.18)
    return jnp.clip(array, -reach, reach).astype(kind)


def setup_inputs(seed: int = 0) -> dict:
    key_list = jax.random.split(jax.random.key(seed), 10)
    query = bell_draw(key_list[0], (DOCUMENT_TOKENS, H * DK), 1.0, 6.0, ((0, 16), (1, 2)))
    keys = draw_keys(jax.random.fold_in(key_list[9], 71), 0)
    values = bell_draw(key_list[2], (DOCUMENT_TOKENS, NH, H * DV), 1.0, 6.0, ((0, 16), (2, 2)))
    beta = draw_beta(jax.random.fold_in(key_list[9], 71), 0)
    gate_log = draw_gate_log(jax.random.fold_in(key_list[9], 71), 0)
    house_count = touch_ends(jax.random.randint(key_list[5], (DOCUMENT_TOKENS,), 1, NH + 1), jax.random.fold_in(key_list[5], 1), 1, NH).astype(jnp.int32)
    out_gate = bell_draw(key_list[6], (DOCUMENT_TOKENS, H * DV), 1.0, 6.0, ((0, 16), (1, 2)))
    norm_gain = jnp.clip(1.0 + 0.18 * jax.random.normal(key_list[7], (DV,), jnp.float32), 0.1, 1.9)
    out_weight = bell_draw(key_list[8], (H * DV, D), (H * DV) ** -0.5, 0.09375, ((1, 2),))
    return {"query": query, "keys": keys, "values": values, "beta": beta, "gate_log": gate_log, "house_count": house_count, "out_gate": out_gate, "norm_gain": norm_gain, "out_weight": out_weight}


epsilon = 1e-06
highest_precision = lax.Precision.HIGHEST

def unit_rows(matrix):
    return matrix / jnp.sqrt(lax.optimization_barrier(jnp.sum(matrix * matrix, axis=-1, keepdims=True)) + epsilon)

def reference(query, keys, values, beta, gate_log, house_count, out_gate, norm_gain, out_weight):
    q_unit = unit_rows(query.astype(jnp.float32).reshape(DOCUMENT_TOKENS, H, DK))
    k_unit = unit_rows(keys.astype(jnp.float32).reshape(DOCUMENT_TOKENS, NH, H, DK))
    value_rows = values.astype(jnp.float32).reshape(DOCUMENT_TOKENS, NH, H, DV)
    active = (jnp.arange(NH, dtype=jnp.int32)[:, None] < house_count[None, :]).astype(jnp.float32)
    strength = (beta * active[:, None, :]).transpose(2, 0, 1)
    forget = jnp.exp(gate_log).T

    def advance(memory_state, inputs):
        current_query, keys_now, values_now, strength_now, forget_now = inputs
        memory_state = memory_state * forget_now[:, None, None]
        for factor_index in range(NH):
            key_vector = keys_now[factor_index]
            retrieved_values = jnp.einsum('dcm,dc->dm', memory_state, key_vector, precision=highest_precision)
            update = values_now[factor_index] - retrieved_values
            memory_state = memory_state + strength_now[factor_index][:, None, None] * key_vector[:, :, None] * update[:, None, :]
        return (memory_state, jnp.einsum('dcm,dc->dm', memory_state, current_query, precision=highest_precision))
    initial = jnp.zeros((H, DK, DV), jnp.float32)
    _, head_out = lax.scan(advance, initial, (q_unit, k_unit, value_rows, strength, forget))
    inverse_rms = 1.0 / jnp.sqrt(lax.optimization_barrier(jnp.mean(head_out * head_out, axis=-1, keepdims=True)) + epsilon)
    gate_vals = jax.nn.silu(out_gate.astype(jnp.float32).reshape(DOCUMENT_TOKENS, H, DV))
    gated = (head_out * inverse_rms * norm_gain * gate_vals).astype(jnp.bfloat16).reshape(DOCUMENT_TOKENS, H * DV)
    return jnp.dot(gated, out_weight, preferred_element_type=jnp.float32).astype(jnp.bfloat16)
```

```python
import functools

import jax
import jax.numpy as jnp
from jax import lax
from jax.experimental import pallas as pl
from jax.experimental.pallas import tpu as pltpu
from jax.sharding import PartitionSpec as P

DK = 128
NH = 2
EPS = 1e-06
F32 = jnp.float32
BF16 = jnp.bfloat16
MESH = pl.DeviceIdType.MESH
MIB = 1024 * 1024


def mm(a, b):
    return jnp.dot(a, b, preferred_element_type=F32)


def mm_t(a, b):
    return lax.dot_general(a, b, (((1,), (1,)), ((), ())), preferred_element_type=F32)


def t_mm(a, b):
    return lax.dot_general(a, b, (((0,), (0,)), ((), ())), preferred_element_type=F32)


def split(x):
    hi = x.astype(BF16)
    return hi, (x - hi.astype(F32)).astype(BF16)


def step_times(shape, axis, tok):
    index = lax.broadcasted_iota(jnp.int32, shape, axis)
    return jnp.where(index < tok, NH * index, NH * (index - tok) + 1)


def prepare(kb, vb, qb, cum_col, cum_row, s_col, s_row):
    tok = qb.shape[0]
    steps = NH * tok
    row_time = step_times((steps, steps), 0, tok)
    col_time = step_times((steps, steps), 1, tok)
    apart = row_time ^ col_time
    strictly = row_time > col_time
    diagonal = row_time == col_time

    gram = mm_t(kb, kb)
    on_diag = jnp.where(diagonal, gram, 0.0)
    rk_row = lax.rsqrt(jnp.sum(on_diag, axis=0, keepdims=True) + EPS)
    rk_col = lax.rsqrt(jnp.sum(on_diag, axis=1, keepdims=True) + EPS)
    qf = qb.astype(F32)
    rq_col = lax.rsqrt(jnp.sum(qf * qf, axis=1, keepdims=True) + EPS)

    small_row = lax.broadcasted_iota(jnp.int32, (tok, tok), 0)
    small_col = lax.broadcasted_iota(jnp.int32, (tok, tok), 1)
    seen = small_row >= small_col
    decay = jnp.where(seen, jnp.exp(jnp.where(seen, cum_col - cum_row, 0.0)), 0.0)
    decay_wide = jnp.concatenate([decay, decay], axis=1)
    decay_full = jnp.concatenate([decay_wide, decay_wide], axis=0)
    cum2_row = jnp.concatenate([cum_row, cum_row], axis=1)
    cum2_col = jnp.concatenate([cum_col, cum_col], axis=0)
    end = cum_row[:, tok - 1 : tok]

    lower = jnp.where(strictly, (s_col * rk_col) * (gram * decay_full) * rk_row, 0.0)
    lower_hi, lower_lo = split(lower)
    unit = jnp.where(diagonal, 1.0, 0.0)
    inverse = unit - jnp.where(apart == 1, lower, 0.0)
    width = 2
    while width < steps:
        corner = jnp.where((apart >= width) & (apart < 2 * width), lower, 0.0).astype(BF16)
        rounded = inverse.astype(BF16)
        inverse = inverse - mm(mm(rounded, corner).astype(BF16), rounded)
        width *= 2
    inv_hi, inv_lo = split(inverse)
    residual = unit - inverse - (mm(lower_hi, inv_hi) + (mm(lower_hi, inv_lo) + mm(lower_lo, inv_hi)))
    inverse = inverse + mm(inv_hi, residual.astype(BF16))

    by_value = inverse * s_row
    val_hi, val_lo = split(by_value)
    key_hi, key_lo = split(by_value * (jnp.exp(cum2_row) * rk_row))
    solved = jnp.concatenate([mm(key_hi, kb) + mm(key_lo, kb), mm(val_hi, vb) + mm(val_lo, vb)], axis=1)
    solved_hi, solved_lo = split(solved)
    faded_hi, faded_lo = split((jnp.exp(end - cum2_col) * rk_col) * solved)
    carried = t_mm(kb, faded_hi) + t_mm(kb, faded_lo)
    mult = jnp.where(small_row == small_col, jnp.exp(end), 0.0) - carried[:, :DK]

    weights = (rq_col * rk_row) * (decay_wide * mm_t(qb, kb))
    w_hi, w_lo = split(weights)
    read = mm(w_hi, solved_hi) + (mm(w_hi, solved_lo) + mm(w_lo, solved_hi))
    query_eff = (jnp.exp(cum_col) * rq_col) * qf - read[:, :DK]
    maps = jnp.concatenate([mult, query_eff], axis=0)
    adds = jnp.concatenate([carried[:, DK:], read[:, DK:]], axis=0)
    return maps, adds


def prepare_kernel(together, k_ref, v_ref, q_ref, cumt_ref, st_ref, cum_ref, s_ref, hi_ref, lo_ref, add_ref):
    def column(ref, head):
        lane = lax.broadcasted_iota(jnp.int32, ref.shape, 1)
        return jnp.sum(jnp.where(lane == head, ref[...], 0.0), axis=1, keepdims=True)

    for i in range(together):
        head = pl.program_id(0) * together + i
        cols = slice(i * DK, (i + 1) * DK)
        maps, adds = prepare(
            k_ref[:, cols], v_ref[:, cols], q_ref[:, cols],
            column(cumt_ref, head), cum_ref[i], column(st_ref, head), s_ref[i],
        )
        hi_ref[i], lo_ref[i] = split(maps)
        add_ref[i] = adds


def relay_kernel(
    n, heads, group, hi_ref, lo_ref, add_ref, gate_ref, gain_ref, w_ref, out_ref,
    w_vmem, arrived, leaving, gated, total,
    w_sem, send_sem, recv_sem, gsend_sem, grecv_sem,
):
    me = lax.axis_index("seq")
    core = lax.axis_index("head")
    tok = gate_ref.shape[1]
    right, left = lax.rem(me + 1, n), lax.rem(me + n - 1, n)
    other = 1 - core

    load = pltpu.make_async_copy(w_ref, w_vmem, w_sem)
    load.start()
    barrier = pltpu.get_barrier_semaphore()
    pl.semaphore_signal(barrier, inc=1, device_id=(left, core), device_id_type=MESH)
    pl.semaphore_signal(barrier, inc=1, device_id=(me, other), device_id_type=MESH)

    @pl.when(me == 0)
    def _():
        arrived[...] = jnp.zeros_like(arrived)

    pl.semaphore_wait(barrier, 2)

    def onward(h):
        return pltpu.make_async_remote_copy(
            src_ref=leaving.at[h], dst_ref=arrived.at[h], send_sem=send_sem.at[h], recv_sem=recv_sem.at[h],
            device_id=(right, core), device_id_type=MESH,
        )

    def across(h):
        slot = gated.at[core * heads + h]
        return pltpu.make_async_remote_copy(
            src_ref=slot, dst_ref=slot, send_sem=gsend_sem.at[h], recv_sem=grecv_sem.at[h],
            device_id=(me, other), device_id_type=MESH,
        )

    @pl.loop(0, heads)
    def _(h):
        @pl.when(me > 0)
        def _():
            onward(h).wait_recv()

        s_hi, s_lo = split(arrived[h])
        both = mm(hi_ref[h], jnp.concatenate([s_hi, s_lo], axis=1))
        result = (both[:, :DK] + (both[:, DK:] + mm(lo_ref[h], s_hi))) + add_ref[h]
        leaving[h] = result[:DK]

        @pl.when(me < n - 1)
        def _():
            onward(h).start()

        rows = result[DK:]
        scale = lax.rsqrt(jnp.mean(rows * rows, axis=1, keepdims=True) + EPS)
        x = gate_ref[h].astype(F32)
        gated[core * heads + h] = (rows * scale * gain_ref[...] * (x / (1.0 + jnp.exp(-x)))).astype(BF16)
        across(h).start()

    load.wait()
    total[...] = jnp.zeros_like(total)

    @pl.loop(0, heads)
    def _(h):
        across(h).wait_recv()

    @pl.loop(0, 2 * heads // group)
    def _(g):
        block = jnp.concatenate([gated[g * group + i] for i in range(group)], axis=1)
        total[...] += mm(block, w_vmem[pl.ds(pl.multiple_of(g * group * DK, group * DK), group * DK), :])

    out_ref[...] = total[...].astype(out_ref.dtype)

    @pl.loop(0, heads)
    def _(h):
        across(h).wait_send()

        @pl.when(me < n - 1)
        def _():
            onward(h).wait_send()


def shards(n, query, keys, values, beta, gate_log, house_count, out_gate, norm_gain, out_weight):
    tok = query.shape[0]
    heads = query.shape[1] // DK
    steps = NH * tok
    width = out_weight.shape[1]
    active = (jnp.arange(NH, dtype=jnp.int32)[:, None] < house_count[None, :]).astype(F32)
    strength = (beta * active[:, None, :]).transpose(1, 0, 2).reshape(heads, steps)
    upper = (jnp.arange(tok)[:, None] <= jnp.arange(tok)[None, :]).astype(F32)
    cum = jnp.dot(gate_log, upper, precision=lax.Precision.HIGHEST)
    k2 = keys.transpose(1, 0, 2).reshape(steps, heads * DK)
    v2 = values.transpose(1, 0, 2).reshape(steps, heads * DK)
    gate3 = out_gate.reshape(tok, heads, DK).transpose(1, 0, 2)

    together = 2
    maps_hi, maps_lo, adds = pl.pallas_call(
        functools.partial(prepare_kernel, together),
        grid=(heads // together,),
        in_specs=[
            pl.BlockSpec((steps, together * DK), lambda i: (0, i)),
            pl.BlockSpec((steps, together * DK), lambda i: (0, i)),
            pl.BlockSpec((tok, together * DK), lambda i: (0, i)),
            pl.BlockSpec((tok, heads), lambda i: (0, 0)),
            pl.BlockSpec((steps, heads), lambda i: (0, 0)),
            pl.BlockSpec((together, 1, tok), lambda i: (i, 0, 0)),
            pl.BlockSpec((together, 1, steps), lambda i: (i, 0, 0)),
        ],
        out_specs=[pl.BlockSpec((together, DK + tok, DK), lambda i: (i, 0, 0))] * 3,
        out_shape=[jax.ShapeDtypeStruct((heads, DK + tok, DK), t) for t in (BF16, BF16, F32)],
        compiler_params=pltpu.CompilerParams(vmem_limit_bytes=40 * MIB),
    )(k2, v2, query, cum.T, strength.T, cum[:, None, :], strength[:, None, :])

    group = 4
    vmem = pl.BlockSpec(memory_space=pltpu.VMEM)
    return pl.pallas_call(
        functools.partial(relay_kernel, n, heads, group),
        in_specs=[vmem] * 5 + [pl.BlockSpec(memory_space=pl.ANY)],
        out_specs=vmem,
        out_shape=jax.ShapeDtypeStruct((tok, width), BF16),
        scratch_shapes=[
            pltpu.VMEM(out_weight.shape, BF16),
            pltpu.VMEM((heads, DK, DK), F32),
            pltpu.VMEM((heads, DK, DK), F32),
            pltpu.VMEM((2 * heads, tok, DK), BF16),
            pltpu.VMEM((tok, width), F32),
            pltpu.SemaphoreType.DMA,
            pltpu.SemaphoreType.DMA((heads,)),
            pltpu.SemaphoreType.DMA((heads,)),
            pltpu.SemaphoreType.DMA((heads,)),
            pltpu.SemaphoreType.DMA((heads,)),
        ],
        compiler_params=pltpu.CompilerParams(
            collective_id=0, has_side_effects=True, vmem_limit_bytes=56 * MIB
        ),
    )(maps_hi, maps_lo, adds, gate3, norm_gain[None, :], out_weight)


def solution(mesh):
    return jax.shard_map(
        functools.partial(shards, mesh.shape["seq"]),
        mesh=mesh,
        in_specs=(
            P("seq", "head"),
            P("seq", None, "head"),
            P("seq", None, "head"),
            P(None, "head", "seq"),
            P("head", "seq"),
            P("seq"),
            P("seq", "head"),
            P(),
            P(None, "head"),
        ),
        out_specs=P("seq", "head"),
        check_vma=False,
    )
```

```python
import functools

import jax
import jax.numpy as jnp
from jax import lax
from jax.experimental import pallas as pl
from jax.experimental.pallas import tpu as pltpu
from jax.sharding import PartitionSpec as P

DK = 128
NH = 2
EPS = 1e-06
F32 = jnp.float32
BF16 = jnp.bfloat16
MESH = pl.DeviceIdType.MESH
MIB = 1024 * 1024


def mm(a, b):
    return jnp.dot(a, b, preferred_element_type=F32)


def mm_t(a, b):
    return lax.dot_general(a, b, (((1,), (1,)), ((), ())), preferred_element_type=F32)


def t_mm(a, b):
    return lax.dot_general(a, b, (((0,), (0,)), ((), ())), preferred_element_type=F32)


def split(x):
    hi = x.astype(BF16)
    return hi, (x - hi.astype(F32)).astype(BF16)


def mm3(a, b):
    return mm(a[0], b[0]) + (mm(a[0], b[1]) + mm(a[1], b[0]))


def prepare(group):
    tok = group[0]["q"].shape[0]
    span = tok
    half = tok // 2
    row_at = lax.broadcasted_iota(jnp.int32, (span, span), 0)
    col_at = lax.broadcasted_iota(jnp.int32, (span, span), 1)

    def time_of(index):
        return jnp.where(index < half, 2 * index, 2 * (index - half) + 1)

    row_time, col_time = time_of(row_at), time_of(col_at)
    apart = row_time ^ col_time
    strictly = row_time > col_time
    diagonal = row_at == col_at
    unit = jnp.where(diagonal, 1.0, 0.0)
    token_at = jnp.where(col_at < half, col_at, col_at - half)
    seen = [row_at >= token_at, row_at >= token_at + half]
    blocks = [slice(0, span), slice(span, 2 * span)]

    lowers, corners, norms = [], [], []
    for x in group:
        k = [x["k"][b] for b in blocks]
        grams = [mm_t(kb, kb) for kb in k]
        cross = mm_t(k[1], k[0])
        on_diag = [jnp.where(diagonal, g, 0.0) for g in grams]
        rk_row = [lax.rsqrt(jnp.sum(d, axis=0, keepdims=True) + EPS) for d in on_diag]
        rk_col = [lax.rsqrt(jnp.sum(d, axis=1, keepdims=True) + EPS) for d in on_diag]
        cr = [x["cum_row"][:, b] for b in blocks]
        cc = [x["cum_col"][b] for b in blocks]
        sc = [x["s_col"][b] for b in blocks]
        for b in range(2):
            fade = jnp.exp(jnp.where(strictly, cc[b] - cr[b], 0.0))
            lowers.append(jnp.where(strictly, (sc[b] * rk_col[b]) * (grams[b] * fade) * rk_row[b], 0.0))
        corners.append((sc[1] * rk_col[1]) * (cross * jnp.exp(cc[1] - cr[0])) * rk_row[0])
        norms.append((rk_row, rk_col, cr, cc, sc))

    inverses = [unit - jnp.where(apart == 1, low, 0.0) for low in lowers]
    width = 2
    while width < span:
        here = (apart >= width) & (apart < 2 * width)
        rounded = [inv.astype(BF16) for inv in inverses]
        firsts = [mm(r, jnp.where(here, low, 0.0).astype(BF16)).astype(BF16) for r, low in zip(rounded, lowers)]
        inverses = [inv - mm(f, r) for inv, f, r in zip(inverses, firsts, rounded)]
        width *= 2
    parts = [split(inv) for inv in inverses]
    residuals = [unit - inv - mm3(split(low), p) for inv, low, p in zip(inverses, lowers, parts)]
    inverses = [inv + mm(p[0], r.astype(BF16)) for inv, p, r in zip(inverses, parts, residuals)]

    firsts = []
    for i, x in enumerate(group):
        rk_row, _, cr, _, _ = norms[i]
        by_value = inverses[2 * i] * x["s_row"][:, blocks[0]]
        val_hi, val_lo = split(by_value)
        key_hi, key_lo = split(by_value * (jnp.exp(cr[0]) * rk_row[0]))
        k, v = x["k"][blocks[0]], x["v"][blocks[0]]
        firsts.append(jnp.concatenate([mm(key_hi, k) + mm(key_lo, k), mm(val_hi, v) + mm(val_lo, v)], axis=1))
    first_parts = [split(f) for f in firsts]
    seconds = []
    for i, x in enumerate(group):
        _, rk_col, _, cc, sc = norms[i]
        k, v = x["k"][blocks[1]].astype(F32), x["v"][blocks[1]].astype(F32)
        right = jnp.concatenate([(sc[1] * jnp.exp(cc[1]) * rk_col[1]) * k, sc[1] * v], axis=1)
        right = right - mm3(split(corners[i]), first_parts[i])
        seconds.append(mm3(split(inverses[2 * i + 1]), split(right)))
    second_parts = [split(s) for s in seconds]

    results = []
    for i, x in enumerate(group):
        rk_row, rk_col, cr, cc, _ = norms[i]
        end = x["cum_row"][:, 2 * span - 1 :]
        ctok = x["cum_tok"]
        q = x["q"]
        qf = q.astype(F32)
        rq = lax.rsqrt(jnp.sum(qf * qf, axis=1, keepdims=True) + EPS)
        mult, add, read = 0.0, 0.0, 0.0
        for b, (whole, pieces) in enumerate([(firsts[i], first_parts[i]), (seconds[i], second_parts[i])]):
            kb = x["k"][blocks[b]]
            faded_hi, faded_lo = split((jnp.exp(end - cc[b]) * rk_col[b]) * whole)
            mult = mult - t_mm(kb, faded_hi[:, :DK])
            add = add + (t_mm(faded_hi[:, DK:], kb) + t_mm(faded_lo[:, DK:], kb))
            lag = jnp.exp(jnp.where(seen[b], ctok - cr[b], 0.0))
            weights = jnp.where(seen[b], (rq * rk_row[b]) * (lag * mm_t(q, kb)), 0.0)
            read = read + mm3(split(weights), pieces)
        query_hi, query_lo = split((jnp.exp(ctok) * rq) * qf - read[:, :DK])
        results.append((mult.astype(BF16), query_hi, query_lo, add, read[:, DK:]))
    return results


def prepare_kernel(together, k_ref, v_ref, q_ref, cumt_ref, ctok_ref, st_ref, cum_ref, s_ref, map_ref, add_ref):
    def column(ref, head):
        lane = lax.broadcasted_iota(jnp.int32, ref.shape, 1)
        return jnp.sum(jnp.where(lane == head, ref[...], 0.0), axis=1, keepdims=True)

    group = []
    for i in range(together):
        head = pl.program_id(0) * together + i
        cols = slice(i * DK, (i + 1) * DK)
        group.append(dict(
            k=k_ref[:, cols], v=v_ref[:, cols], q=q_ref[:, cols],
            cum_col=column(cumt_ref, head), cum_tok=column(ctok_ref, head), s_col=column(st_ref, head),
            cum_row=cum_ref[i], s_row=s_ref[i],
        ))
    for i, (mult, query_hi, query_lo, add, local) in enumerate(prepare(group)):
        map_ref[i, 0], map_ref[i, 1], map_ref[i, 2] = mult, query_hi, query_lo
        add_ref[i, 0], add_ref[i, 1] = add, local


def relay_kernel(
    n, heads, group, map_hbm, add_hbm, gate_ref, end_ref, gain_ref, w_ref, out_ref,
    w_vmem, maps, adds, arrived, leaving, gated, total,
    w_sem, map_sem, add_sem, send_sem, recv_sem, gsend_sem, grecv_sem,
):
    me = lax.axis_index("seq")
    core = lax.axis_index("head")
    right, left = lax.rem(me + 1, n), lax.rem(me + n - 1, n)
    other = 1 - core
    part = DK // 2

    def load_map(h):
        return pltpu.make_async_copy(map_hbm.at[h], maps.at[h], map_sem.at[h])

    def load_add(h):
        return pltpu.make_async_copy(add_hbm.at[h], adds.at[h], add_sem.at[h])

    @pl.loop(0, heads)
    def _(h):
        load_map(h).start()
        load_add(h).start()

    load = pltpu.make_async_copy(w_ref, w_vmem, w_sem)
    load.start()
    barrier = pltpu.get_barrier_semaphore()
    pl.semaphore_signal(barrier, inc=1, device_id=(left, core), device_id_type=MESH)
    pl.semaphore_signal(barrier, inc=1, device_id=(me, other), device_id_type=MESH)

    @pl.when(me == 0)
    def _():
        arrived[...] = jnp.zeros_like(arrived)

    pl.semaphore_wait(barrier, 2)

    def onward(h, i):
        return pltpu.make_async_remote_copy(
            src_ref=leaving.at[2 * h + i], dst_ref=arrived.at[2 * h + i],
            send_sem=send_sem.at[2 * h + i], recv_sem=recv_sem.at[2 * h + i],
            device_id=(right, core), device_id_type=MESH,
        )

    def across(h):
        slot = gated.at[core * heads + h]
        return pltpu.make_async_remote_copy(
            src_ref=slot, dst_ref=slot, send_sem=gsend_sem.at[h], recv_sem=grecv_sem.at[h],
            device_id=(me, other), device_id_type=MESH,
        )

    @pl.loop(0, heads)
    def _(h):
        load_map(h).wait()
        load_add(h).wait()
        end = end_ref[h]
        for i in range(2):

            @pl.when(me > 0)
            def _():
                onward(h, i).wait_recv()

            state = arrived[2 * h + i]
            moved = mm_t(state.astype(BF16), maps[h, 0])
            leaving[2 * h + i] = (end * state + adds[h, 0, i * part : (i + 1) * part]) + moved

            @pl.when(me < n - 1)
            def _():
                onward(h, i).start()

        s_hi, s_lo = split(jnp.concatenate([arrived[2 * h], arrived[2 * h + 1]], axis=0))
        rows = mm_t(maps[h, 1], s_hi) + (mm_t(maps[h, 1], s_lo) + mm_t(maps[h, 2], s_hi)) + adds[h, 1]
        scale = lax.rsqrt(jnp.mean(rows * rows, axis=1, keepdims=True) + EPS)
        x = gate_ref[:, pl.ds(pl.multiple_of(h * DK, DK), DK)].astype(F32)
        gated[core * heads + h] = (rows * scale * gain_ref[...] * (x / (1.0 + jnp.exp(-x)))).astype(BF16)
        across(h).start()

    load.wait()

    def project(base):
        block = jnp.concatenate([gated[base + i] for i in range(group)], axis=1)
        start = pl.multiple_of(base * DK, group * DK)
        return mm(block, w_vmem[pl.ds(start, group * DK), :])

    total[...] = project(core * heads)

    @pl.loop(1, heads // group)
    def _(g):
        total[...] += project(core * heads + g * group)

    @pl.loop(0, heads // group)
    def _(g):
        for i in range(group):
            across(g * group + i).wait_recv()
        total[...] += project(other * heads + g * group)

    out_ref[...] = total[...].astype(out_ref.dtype)

    @pl.loop(0, heads)
    def _(h):
        across(h).wait_send()

        @pl.when(me < n - 1)
        def _():
            onward(h, 0).wait_send()
            onward(h, 1).wait_send()


def shards(n, query, keys, values, beta, gate_log, house_count, out_gate, norm_gain, out_weight):
    tok = query.shape[0]
    heads = query.shape[1] // DK
    steps = NH * tok
    half = tok // 2
    width = out_weight.shape[1]
    active = (jnp.arange(NH, dtype=jnp.int32)[:, None] < house_count[None, :]).astype(F32)
    strength = (beta * active[:, None, :]).reshape(NH, heads, 2, half).transpose(1, 2, 0, 3).reshape(heads, steps)
    upper = (jnp.arange(tok)[:, None] <= jnp.arange(tok)[None, :]).astype(F32)
    cum = jnp.dot(gate_log, upper, precision=lax.Precision.HIGHEST)
    cum_steps = jnp.broadcast_to(cum.reshape(heads, 2, 1, half), (heads, 2, NH, half)).reshape(heads, steps)
    k2 = keys.reshape(2, half, NH, heads * DK).transpose(0, 2, 1, 3).reshape(steps, heads * DK)
    v2 = values.reshape(2, half, NH, heads * DK).transpose(0, 2, 1, 3).reshape(steps, heads * DK)
    ends = jnp.broadcast_to(jnp.exp(cum[:, tok - 1 :])[:, :, None], (heads, 1, DK))

    together = 4
    maps, adds = pl.pallas_call(
        functools.partial(prepare_kernel, together),
        grid=(heads // together,),
        in_specs=[
            pl.BlockSpec((steps, together * DK), lambda i: (0, i)),
            pl.BlockSpec((steps, together * DK), lambda i: (0, i)),
            pl.BlockSpec((tok, together * DK), lambda i: (0, i)),
            pl.BlockSpec((steps, heads), lambda i: (0, 0)),
            pl.BlockSpec((tok, heads), lambda i: (0, 0)),
            pl.BlockSpec((steps, heads), lambda i: (0, 0)),
            pl.BlockSpec((together, 1, steps), lambda i: (i, 0, 0)),
            pl.BlockSpec((together, 1, steps), lambda i: (i, 0, 0)),
        ],
        out_specs=[
            pl.BlockSpec((together, 3, tok, DK), lambda i: (i, 0, 0, 0)),
            pl.BlockSpec((together, 2, tok, DK), lambda i: (i, 0, 0, 0)),
        ],
        out_shape=[
            jax.ShapeDtypeStruct((heads, 3, tok, DK), BF16),
            jax.ShapeDtypeStruct((heads, 2, tok, DK), F32),
        ],
        compiler_params=pltpu.CompilerParams(vmem_limit_bytes=40 * MIB),
    )(k2, v2, query, cum_steps.T, cum.T, strength.T, cum_steps[:, None, :], strength[:, None, :])

    group = 4
    vmem = pl.BlockSpec(memory_space=pltpu.VMEM)
    hbm = pl.BlockSpec(memory_space=pl.ANY)
    return pl.pallas_call(
        functools.partial(relay_kernel, n, heads, group),
        in_specs=[hbm, hbm, vmem, vmem, vmem, hbm],
        out_specs=vmem,
        out_shape=jax.ShapeDtypeStruct((tok, width), BF16),
        scratch_shapes=[
            pltpu.VMEM(out_weight.shape, BF16),
            pltpu.VMEM((heads, 3, tok, DK), BF16),
            pltpu.VMEM((heads, 2, tok, DK), F32),
            pltpu.VMEM((2 * heads, DK // 2, DK), F32),
            pltpu.VMEM((2 * heads, DK // 2, DK), F32),
            pltpu.VMEM((2 * heads, tok, DK), BF16),
            pltpu.VMEM((tok, width), F32),
            pltpu.SemaphoreType.DMA,
            pltpu.SemaphoreType.DMA((heads,)),
            pltpu.SemaphoreType.DMA((heads,)),
            pltpu.SemaphoreType.DMA((2 * heads,)),
            pltpu.SemaphoreType.DMA((2 * heads,)),
            pltpu.SemaphoreType.DMA((heads,)),
            pltpu.SemaphoreType.DMA((heads,)),
        ],
        compiler_params=pltpu.CompilerParams(
            collective_id=0, has_side_effects=True, vmem_limit_bytes=56 * MIB
        ),
    )(maps, adds, out_gate, ends, norm_gain[None, :], out_weight)


def solution(mesh):
    return jax.shard_map(
        functools.partial(shards, mesh.shape["seq"]),
        mesh=mesh,
        in_specs=(
            P("seq", "head"),
            P("seq", None, "head"),
            P("seq", None, "head"),
            P(None, "head", "seq"),
            P("head", "seq"),
            P("seq"),
            P("seq", "head"),
            P(),
            P(None, "head"),
        ),
        out_specs=P("seq", "head"),
        check_vma=False,
    )
```

```python
import functools

import jax
import jax.numpy as jnp
from jax import lax
from jax.experimental import pallas as pl
from jax.experimental.pallas import tpu as pltpu
from jax.sharding import PartitionSpec as P

DK = 128
NH = 2
EPS = 1e-06
F32 = jnp.float32
BF16 = jnp.bfloat16
MESH = pl.DeviceIdType.MESH
MIB = 1024 * 1024


def mm(a, b):
    return jnp.dot(a, b, preferred_element_type=F32)


def mm_t(a, b):
    return lax.dot_general(a, b, (((1,), (1,)), ((), ())), preferred_element_type=F32)


def t_mm(a, b):
    return lax.dot_general(a, b, (((0,), (0,)), ((), ())), preferred_element_type=F32)


def split(x):
    hi = x.astype(BF16)
    return hi, (x - hi.astype(F32)).astype(BF16)


def mm3(a, b):
    return mm(a[0], b[0]) + (mm(a[0], b[1]) + mm(a[1], b[0]))


def prepare(group):
    tok = group[0]["q"].shape[0]
    span = tok
    half = tok // 2
    row_at = lax.broadcasted_iota(jnp.int32, (span, span), 0)
    col_at = lax.broadcasted_iota(jnp.int32, (span, span), 1)

    def time_of(index):
        return jnp.where(index < half, 2 * index, 2 * (index - half) + 1)

    row_time, col_time = time_of(row_at), time_of(col_at)
    apart = row_time ^ col_time
    strictly = row_time > col_time
    diagonal = row_at == col_at
    unit = jnp.where(diagonal, 1.0, 0.0)
    token_at = jnp.where(col_at < half, col_at, col_at - half)
    seen = [row_at >= token_at, row_at >= token_at + half]
    blocks = [slice(0, span), slice(span, 2 * span)]

    lowers, corners, norms = [], [], []
    for x in group:
        k = [x["k"][b] for b in blocks]
        grams = [mm_t(kb, kb) for kb in k]
        cross = mm_t(k[1], k[0])
        on_diag = [jnp.where(diagonal, g, 0.0) for g in grams]
        rk_row = [lax.rsqrt(jnp.sum(d, axis=0, keepdims=True) + EPS) for d in on_diag]
        rk_col = [lax.rsqrt(jnp.sum(d, axis=1, keepdims=True) + EPS) for d in on_diag]
        cr = [x["cum_row"][:, b] for b in blocks]
        cc = [x["cum_col"][b] for b in blocks]
        sc = [x["s_col"][b] for b in blocks]
        for b in range(2):
            fade = jnp.exp(jnp.where(strictly, cc[b] - cr[b], 0.0))
            lowers.append(jnp.where(strictly, (sc[b] * rk_col[b]) * (grams[b] * fade) * rk_row[b], 0.0))
        corners.append((sc[1] * rk_col[1]) * (cross * jnp.exp(cc[1] - cr[0])) * rk_row[0])
        norms.append((rk_row, rk_col, cr, cc, sc))

    inverses = [unit - jnp.where(apart == 1, low, 0.0) for low in lowers]
    width = 2
    while width < span:
        here = (apart >= width) & (apart < 2 * width)
        rounded = [inv.astype(BF16) for inv in inverses]
        firsts = [mm(r, jnp.where(here, low, 0.0).astype(BF16)).astype(BF16) for r, low in zip(rounded, lowers)]
        inverses = [inv - mm(f, r) for inv, f, r in zip(inverses, firsts, rounded)]
        width *= 2
    parts = [split(inv) for inv in inverses]
    residuals = [unit - inv - mm3(split(low), p) for inv, low, p in zip(inverses, lowers, parts)]
    inverses = [inv + mm(p[0], r.astype(BF16)) for inv, p, r in zip(inverses, parts, residuals)]

    firsts = []
    for i, x in enumerate(group):
        rk_row, _, cr, _, _ = norms[i]
        by_value = inverses[2 * i] * x["s_row"][:, blocks[0]]
        val_hi, val_lo = split(by_value)
        key_hi, key_lo = split(by_value * (jnp.exp(cr[0]) * rk_row[0]))
        k, v = x["k"][blocks[0]], x["v"][blocks[0]]
        firsts.append(jnp.concatenate([mm(key_hi, k) + mm(key_lo, k), mm(val_hi, v) + mm(val_lo, v)], axis=1))
    first_parts = [split(f) for f in firsts]
    seconds = []
    for i, x in enumerate(group):
        _, rk_col, _, cc, sc = norms[i]
        k, v = x["k"][blocks[1]].astype(F32), x["v"][blocks[1]].astype(F32)
        right = jnp.concatenate([(sc[1] * jnp.exp(cc[1]) * rk_col[1]) * k, sc[1] * v], axis=1)
        right = right - mm3(split(corners[i]), first_parts[i])
        seconds.append(mm3(split(inverses[2 * i + 1]), split(right)))
    second_parts = [split(s) for s in seconds]

    results = []
    for i, x in enumerate(group):
        rk_row, rk_col, cr, cc, _ = norms[i]
        end = x["cum_row"][:, 2 * span - 1 :]
        ctok = x["cum_tok"]
        q = x["q"]
        qf = q.astype(F32)
        rq = lax.rsqrt(jnp.sum(qf * qf, axis=1, keepdims=True) + EPS)
        mult, add, read = 0.0, 0.0, 0.0
        for b, (whole, pieces) in enumerate([(firsts[i], first_parts[i]), (seconds[i], second_parts[i])]):
            kb = x["k"][blocks[b]]
            faded_hi, faded_lo = split((jnp.exp(end - cc[b]) * rk_col[b]) * whole)
            mult = mult - t_mm(kb, faded_hi[:, :DK])
            add = add + (t_mm(faded_hi[:, DK:], kb) + t_mm(faded_lo[:, DK:], kb))
            lag = jnp.exp(jnp.where(seen[b], ctok - cr[b], 0.0))
            weights = jnp.where(seen[b], (rq * rk_row[b]) * (lag * mm_t(q, kb)), 0.0)
            read = read + mm3(split(weights), pieces)
        query_hi, query_lo = split((jnp.exp(ctok) * rq) * qf - read[:, :DK])
        results.append((mult.astype(BF16), add.astype(BF16), query_hi, query_lo, add, read[:, DK:]))
    return results


def prepare_kernel(together, k_ref, v_ref, q_ref, cumt_ref, ctok_ref, st_ref, cum_ref, s_ref, map_ref, add_ref):
    def column(ref, head):
        lane = lax.broadcasted_iota(jnp.int32, ref.shape, 1)
        return jnp.sum(jnp.where(lane == head, ref[...], 0.0), axis=1, keepdims=True)

    group = []
    for i in range(together):
        head = pl.program_id(0) * together + i
        cols = slice(i * DK, (i + 1) * DK)
        group.append(dict(
            k=k_ref[:, cols], v=v_ref[:, cols], q=q_ref[:, cols],
            cum_col=column(cumt_ref, head), cum_tok=column(ctok_ref, head), s_col=column(st_ref, head),
            cum_row=cum_ref[i], s_row=s_ref[i],
        ))
    for i, (mult, add_low, query_hi, query_lo, add, local) in enumerate(prepare(group)):
        map_ref[i, 0], map_ref[i, 1] = mult, add_low
        map_ref[i, 2], map_ref[i, 3] = query_hi, query_lo
        add_ref[i, 0], add_ref[i, 1] = add, local


def relay_kernel(
    n, heads, group, map_hbm, add_hbm, gate_ref, end_ref, gain_ref, w_ref, out_ref,
    w_vmem, maps, adds, mates, mate_end, joint_map, joint_add, arrived, leaving, own, gated, total,
    w_sem, map_sem, add_sem, end_sem, mate_send, mate_recv, send_sem, recv_sem, gsend_sem, grecv_sem,
):
    me = lax.axis_index("seq")
    core = lax.axis_index("head")
    odd = lax.rem(me, 2)
    first = me - odd
    mate = me + 1 - 2 * odd
    after, before = lax.rem(first + 2, n), lax.rem(first + n - 2, n)
    other = 1 - core
    part = DK // 2
    relays = (odd == 0) & (me < n - 2)

    def load_map(h):
        return pltpu.make_async_copy(map_hbm.at[h], maps.at[h], map_sem.at[h])

    def load_add(h):
        return pltpu.make_async_copy(add_hbm.at[h], adds.at[h], add_sem.at[h])

    def swap_end():
        return pltpu.make_async_remote_copy(
            src_ref=end_ref, dst_ref=mate_end, send_sem=end_sem.at[0], recv_sem=end_sem.at[1],
            device_id=(mate, core), device_id_type=MESH,
        )

    def swap(h):
        return pltpu.make_async_remote_copy(
            src_ref=map_hbm.at[h, pl.ds(0, 2)], dst_ref=mates.at[h], send_sem=mate_send.at[h], recv_sem=mate_recv.at[h],
            device_id=(mate, core), device_id_type=MESH,
        )

    def onward(h, i, to):
        return pltpu.make_async_remote_copy(
            src_ref=leaving.at[2 * h + i], dst_ref=arrived.at[2 * h + i],
            send_sem=send_sem.at[to, 2 * h + i], recv_sem=recv_sem.at[2 * h + i],
            device_id=(after + to, core), device_id_type=MESH,
        )

    def across(h):
        slot = gated.at[core * heads + h]
        return pltpu.make_async_remote_copy(
            src_ref=slot, dst_ref=slot, send_sem=gsend_sem.at[h], recv_sem=grecv_sem.at[h],
            device_id=(me, other), device_id_type=MESH,
        )

    barrier = pltpu.get_barrier_semaphore()
    pl.semaphore_signal(barrier, inc=1, device_id=(mate, core), device_id_type=MESH)
    pl.semaphore_signal(barrier, inc=1, device_id=(me, other), device_id_type=MESH)
    pl.semaphore_signal(barrier, inc=1, device_id=(before, core), device_id_type=MESH)

    @pl.loop(0, heads)
    def _(h):
        load_map(h).start()
        load_add(h).start()

    @pl.when(me < 2)
    def _():
        arrived[...] = jnp.zeros_like(arrived)

    pl.semaphore_wait(barrier, 4 - 2 * odd)
    swap_end().start()

    @pl.loop(0, heads)
    def _(h):
        swap(h).start()

    load = pltpu.make_async_copy(w_ref, w_vmem, w_sem)
    load.start()

    def ready(h):
        load_map(h).wait()
        load_add(h).wait()
        swap(h).wait_recv()

    def join(h):
        mine, theirs = maps[h, 0], mates[h, 0]
        mine_end, theirs_end = end_ref[h], mate_end[h]
        add = adds[h, 0]
        joint_map[h] = (
            theirs_end * mine.astype(F32) + mine_end * theirs.astype(F32) + mm(theirs, mine)
        ).astype(BF16)
        joint_add[h] = theirs_end * add + mm_t(add.astype(BF16), theirs) + mates[h, 1].astype(F32)

    swap_end().wait_recv()
    ready(0)
    join(0)

    @pl.loop(0, heads)
    def _(h):
        for i in range(2):

            @pl.when(me > 1)
            def _():
                onward(h, i, 0).wait_recv()

            @pl.when(relays)
            def _():
                state = arrived[2 * h + i]
                moved = mm_t(state.astype(BF16), joint_map[h])
                end = end_ref[h] * mate_end[h]
                leaving[2 * h + i] = (end * state + joint_add[h, i * part : (i + 1) * part]) + moved
                onward(h, i, 0).start()
                onward(h, i, 1).start()

        @pl.when(odd == 0)
        def _():
            own[:part] = arrived[2 * h]
            own[part:] = arrived[2 * h + 1]

        @pl.when(odd == 1)
        def _():
            state = jnp.concatenate([arrived[2 * h], arrived[2 * h + 1]], axis=0)
            own[...] = mate_end[h] * state + mm_t(state.astype(BF16), mates[h, 0]) + mates[h, 1].astype(F32)

        @pl.when(h < heads - 1)
        def _():
            ready(h + 1)

        join(lax.rem(h + 1, heads))
        s_hi, s_lo = split(own[...])
        rows = mm_t(maps[h, 2], s_hi) + (mm_t(maps[h, 2], s_lo) + mm_t(maps[h, 3], s_hi)) + adds[h, 1]
        scale = lax.rsqrt(jnp.mean(rows * rows, axis=1, keepdims=True) + EPS)
        x = gate_ref[:, pl.ds(pl.multiple_of(h * DK, DK), DK)].astype(F32)
        gated[core * heads + h] = (rows * scale * gain_ref[...] * (x / (1.0 + jnp.exp(-x)))).astype(BF16)
        across(h).start()

    load.wait()

    def project(base):
        block = jnp.concatenate([gated[base + i] for i in range(group)], axis=1)
        start = pl.multiple_of(base * DK, group * DK)
        return mm(block, w_vmem[pl.ds(start, group * DK), :])

    total[...] = project(core * heads)

    @pl.loop(1, heads // group)
    def _(g):
        total[...] += project(core * heads + g * group)

    @pl.loop(0, heads // group)
    def _(g):
        for i in range(group):
            across(g * group + i).wait_recv()
        total[...] += project(other * heads + g * group)

    out_ref[...] = total[...].astype(out_ref.dtype)

    @pl.loop(0, heads)
    def _(h):
        across(h).wait_send()
        swap(h).wait_send()

        @pl.when(relays)
        def _():
            for i in range(2):
                onward(h, i, 0).wait_send()
                onward(h, i, 1).wait_send()

    swap_end().wait_send()


def shards(n, query, keys, values, beta, gate_log, house_count, out_gate, norm_gain, out_weight):
    tok = query.shape[0]
    heads = query.shape[1] // DK
    steps = NH * tok
    half = tok // 2
    width = out_weight.shape[1]
    active = (jnp.arange(NH, dtype=jnp.int32)[:, None] < house_count[None, :]).astype(F32)
    strength = (beta * active[:, None, :]).reshape(NH, heads, 2, half).transpose(1, 2, 0, 3).reshape(heads, steps)
    upper = (jnp.arange(tok)[:, None] <= jnp.arange(tok)[None, :]).astype(F32)
    cum = jnp.dot(gate_log, upper, precision=lax.Precision.HIGHEST)
    cum_steps = jnp.broadcast_to(cum.reshape(heads, 2, 1, half), (heads, 2, NH, half)).reshape(heads, steps)
    k2 = keys.reshape(2, half, NH, heads * DK).transpose(0, 2, 1, 3).reshape(steps, heads * DK)
    v2 = values.reshape(2, half, NH, heads * DK).transpose(0, 2, 1, 3).reshape(steps, heads * DK)
    ends = jnp.broadcast_to(jnp.exp(cum[:, tok - 1 :])[:, :, None], (heads, 1, DK))

    together = 4
    maps, adds = pl.pallas_call(
        functools.partial(prepare_kernel, together),
        grid=(heads // together,),
        in_specs=[
            pl.BlockSpec((steps, together * DK), lambda i: (0, i)),
            pl.BlockSpec((steps, together * DK), lambda i: (0, i)),
            pl.BlockSpec((tok, together * DK), lambda i: (0, i)),
            pl.BlockSpec((steps, heads), lambda i: (0, 0)),
            pl.BlockSpec((tok, heads), lambda i: (0, 0)),
            pl.BlockSpec((steps, heads), lambda i: (0, 0)),
            pl.BlockSpec((together, 1, steps), lambda i: (i, 0, 0)),
            pl.BlockSpec((together, 1, steps), lambda i: (i, 0, 0)),
        ],
        out_specs=[
            pl.BlockSpec((together, 4, tok, DK), lambda i: (i, 0, 0, 0)),
            pl.BlockSpec((together, 2, tok, DK), lambda i: (i, 0, 0, 0)),
        ],
        out_shape=[
            jax.ShapeDtypeStruct((heads, 4, tok, DK), BF16),
            jax.ShapeDtypeStruct((heads, 2, tok, DK), F32),
        ],
        compiler_params=pltpu.CompilerParams(vmem_limit_bytes=61 * MIB),
    )(k2, v2, query, cum_steps.T, cum.T, strength.T, cum_steps[:, None, :], strength[:, None, :])

    group = 4
    vmem = pl.BlockSpec(memory_space=pltpu.VMEM)
    hbm = pl.BlockSpec(memory_space=pltpu.HBM)
    return pl.pallas_call(
        functools.partial(relay_kernel, n, heads, group),
        in_specs=[hbm, hbm, vmem, vmem, vmem, hbm],
        out_specs=vmem,
        out_shape=jax.ShapeDtypeStruct((tok, width), BF16),
        scratch_shapes=[
            pltpu.VMEM(out_weight.shape, BF16),
            pltpu.VMEM((heads, 4, tok, DK), BF16),
            pltpu.VMEM((heads, 2, tok, DK), F32),
            pltpu.VMEM((heads, 2, DK, DK), BF16),
            pltpu.VMEM(ends.shape, F32),
            pltpu.VMEM((heads, DK, DK), BF16),
            pltpu.VMEM((heads, DK, DK), F32),
            pltpu.VMEM((2 * heads, DK // 2, DK), F32),
            pltpu.VMEM((2 * heads, DK // 2, DK), F32),
            pltpu.VMEM((DK, DK), F32),
            pltpu.VMEM((2 * heads, tok, DK), BF16),
            pltpu.VMEM((tok, width), F32),
            pltpu.SemaphoreType.DMA,
            pltpu.SemaphoreType.DMA((heads,)),
            pltpu.SemaphoreType.DMA((heads,)),
            pltpu.SemaphoreType.DMA((2,)),
            pltpu.SemaphoreType.DMA((heads,)),
            pltpu.SemaphoreType.DMA((heads,)),
            pltpu.SemaphoreType.DMA((2, 2 * heads)),
            pltpu.SemaphoreType.DMA((2 * heads,)),
            pltpu.SemaphoreType.DMA((heads,)),
            pltpu.SemaphoreType.DMA((heads,)),
        ],
        compiler_params=pltpu.CompilerParams(
            collective_id=0, has_side_effects=True, vmem_limit_bytes=56 * MIB
        ),
    )(maps, adds, out_gate, ends, norm_gain[None, :], out_weight)


def solution(mesh):
    return jax.shard_map(
        functools.partial(shards, mesh.shape["seq"]),
        mesh=mesh,
        in_specs=(
            P("seq", "head"),
            P("seq", None, "head"),
            P("seq", None, "head"),
            P(None, "head", "seq"),
            P("head", "seq"),
            P("seq"),
            P("seq", "head"),
            P(),
            P(None, "head"),
        ),
        out_specs=P("seq", "head"),
        check_vma=False,
    )
```

```python
import functools

import jax
import jax.numpy as jnp
from jax import lax
from jax.experimental import pallas as pl
from jax.experimental.pallas import tpu as pltpu
from jax.sharding import PartitionSpec as P

DK = 128
NH = 2
EPS = 1e-06
F32 = jnp.float32
BF16 = jnp.bfloat16
MESH = pl.DeviceIdType.MESH
MIB = 1024 * 1024


def mm(a, b):
    return jnp.dot(a, b, preferred_element_type=F32)


def mm_t(a, b):
    return lax.dot_general(a, b, (((1,), (1,)), ((), ())), preferred_element_type=F32)


def t_mm(a, b):
    return lax.dot_general(a, b, (((0,), (0,)), ((), ())), preferred_element_type=F32)


def split(x):
    hi = x.astype(BF16)
    return hi, (x - hi.astype(F32)).astype(BF16)


def mm3(a, b):
    return mm(a[0], b[0]) + (mm(a[0], b[1]) + mm(a[1], b[0]))


def prepare(group):
    tok = group[0]["q"].shape[0]
    span = tok
    half = tok // 2
    row_at = lax.broadcasted_iota(jnp.int32, (span, span), 0)
    col_at = lax.broadcasted_iota(jnp.int32, (span, span), 1)

    def time_of(index):
        return jnp.where(index < half, 2 * index, 2 * (index - half) + 1)

    row_time, col_time = time_of(row_at), time_of(col_at)
    apart = row_time ^ col_time
    strictly = row_time > col_time
    diagonal = row_at == col_at
    unit = jnp.where(diagonal, 1.0, 0.0)
    token_at = jnp.where(col_at < half, col_at, col_at - half)
    seen = [row_at >= token_at, row_at >= token_at + half]
    blocks = [slice(0, span), slice(span, 2 * span)]

    lowers, corners, norms = [], [], []
    for x in group:
        k = [x["k"][b] for b in blocks]
        grams = [mm_t(kb, kb) for kb in k]
        cross = mm_t(k[1], k[0])
        on_diag = [jnp.where(diagonal, g, 0.0) for g in grams]
        rk_row = [lax.rsqrt(jnp.sum(d, axis=0, keepdims=True) + EPS) for d in on_diag]
        rk_col = [lax.rsqrt(jnp.sum(d, axis=1, keepdims=True) + EPS) for d in on_diag]
        cr = [x["cum_row"][:, b] for b in blocks]
        cc = [x["cum_col"][b] for b in blocks]
        sc = [x["s_col"][b] for b in blocks]
        for b in range(2):
            fade = jnp.exp(jnp.where(strictly, cc[b] - cr[b], 0.0))
            lowers.append(jnp.where(strictly, (sc[b] * rk_col[b]) * (grams[b] * fade) * rk_row[b], 0.0))
        corners.append((sc[1] * rk_col[1]) * (cross * jnp.exp(cc[1] - cr[0])) * rk_row[0])
        norms.append((rk_row, rk_col, cr, cc, sc))

    inverses = [unit - jnp.where(apart == 1, low, 0.0) for low in lowers]
    width = 2
    while width < span:
        here = (apart >= width) & (apart < 2 * width)
        rounded = [inv.astype(BF16) for inv in inverses]
        firsts = [mm(r, jnp.where(here, low, 0.0).astype(BF16)).astype(BF16) for r, low in zip(rounded, lowers)]
        inverses = [inv - mm(f, r) for inv, f, r in zip(inverses, firsts, rounded)]
        width *= 2
    parts = [split(inv) for inv in inverses]
    residuals = [unit - inv - mm3(split(low), p) for inv, low, p in zip(inverses, lowers, parts)]
    inverses = [inv + mm(p[0], r.astype(BF16)) for inv, p, r in zip(inverses, parts, residuals)]

    firsts = []
    for i, x in enumerate(group):
        rk_row, _, cr, _, _ = norms[i]
        by_value = inverses[2 * i] * x["s_row"][:, blocks[0]]
        val_hi, val_lo = split(by_value)
        key_hi, key_lo = split(by_value * (jnp.exp(cr[0]) * rk_row[0]))
        k, v = x["k"][blocks[0]], x["v"][blocks[0]]
        firsts.append(jnp.concatenate([mm(key_hi, k) + mm(key_lo, k), mm(val_hi, v) + mm(val_lo, v)], axis=1))
    first_parts = [split(f) for f in firsts]
    seconds = []
    for i, x in enumerate(group):
        _, rk_col, _, cc, sc = norms[i]
        k, v = x["k"][blocks[1]].astype(F32), x["v"][blocks[1]].astype(F32)
        right = jnp.concatenate([(sc[1] * jnp.exp(cc[1]) * rk_col[1]) * k, sc[1] * v], axis=1)
        right = right - mm3(split(corners[i]), first_parts[i])
        seconds.append(mm3(split(inverses[2 * i + 1]), split(right)))
    second_parts = [split(s) for s in seconds]

    results = []
    for i, x in enumerate(group):
        rk_row, rk_col, cr, cc, _ = norms[i]
        end = x["cum_row"][:, 2 * span - 1 :]
        ctok = x["cum_tok"]
        q = x["q"]
        qf = q.astype(F32)
        rq = lax.rsqrt(jnp.sum(qf * qf, axis=1, keepdims=True) + EPS)
        mult, add, read = 0.0, 0.0, 0.0
        for b, (whole, pieces) in enumerate([(firsts[i], first_parts[i]), (seconds[i], second_parts[i])]):
            kb = x["k"][blocks[b]]
            faded_hi, faded_lo = split((jnp.exp(end - cc[b]) * rk_col[b]) * whole)
            mult = mult - t_mm(kb, faded_hi[:, :DK])
            add = add + (t_mm(faded_hi[:, DK:], kb) + t_mm(faded_lo[:, DK:], kb))
            lag = jnp.exp(jnp.where(seen[b], ctok - cr[b], 0.0))
            weights = jnp.where(seen[b], (rq * rk_row[b]) * (lag * mm_t(q, kb)), 0.0)
            read = read + mm3(split(weights), pieces)
        query_hi, query_lo = split((jnp.exp(ctok) * rq) * qf - read[:, :DK])
        results.append((mult.astype(BF16), add.astype(BF16), query_hi, query_lo, add, read[:, DK:]))
    return results


def prepare_kernel(together, k_ref, v_ref, q_ref, cumt_ref, ctok_ref, st_ref, cum_ref, s_ref, map_ref, add_ref):
    def column(ref, head):
        lane = lax.broadcasted_iota(jnp.int32, ref.shape, 1)
        return jnp.sum(jnp.where(lane == head, ref[...], 0.0), axis=1, keepdims=True)

    group = []
    for i in range(together):
        head = pl.program_id(0) * together + i
        cols = slice(i * DK, (i + 1) * DK)
        group.append(dict(
            k=k_ref[:, cols], v=v_ref[:, cols], q=q_ref[:, cols],
            cum_col=column(cumt_ref, head), cum_tok=column(ctok_ref, head), s_col=column(st_ref, head),
            cum_row=cum_ref[i], s_row=s_ref[i],
        ))
    for i, (mult, add_low, query_hi, query_lo, add, local) in enumerate(prepare(group)):
        map_ref[i, 0], map_ref[i, 1] = mult, add_low
        map_ref[i, 2], map_ref[i, 3] = query_hi, query_lo
        add_ref[i, 0], add_ref[i, 1] = add, local


def relay_kernel(
    n, heads, group, map_hbm, add_hbm, gate_ref, end_ref, gain_ref, w_ref, out_ref,
    w_vmem, maps, adds, mates, mate_end, joint_map, joint_add, arrived, leaving, passing, gated, total,
    w_sem, map_sem, add_sem, end_sem, mate_send, mate_recv, send_sem, pass_sem, recv_sem, gsend_sem, grecv_sem,
):
    me = lax.axis_index("seq")
    core = lax.axis_index("head")
    odd = lax.rem(me, 2)
    first = me - odd
    mate = me + 1 - 2 * odd
    after, before = lax.rem(first + 2, n), lax.rem(first + n - 2, n)
    other = 1 - core
    part = DK // 2
    relays = (odd == 0) & (me < n - 2)

    def load_map(h):
        return pltpu.make_async_copy(map_hbm.at[h], maps.at[h], map_sem.at[h])

    def load_add(h):
        return pltpu.make_async_copy(add_hbm.at[h], adds.at[h], add_sem.at[h])

    def swap_end():
        return pltpu.make_async_remote_copy(
            src_ref=end_ref, dst_ref=mate_end, send_sem=end_sem.at[0], recv_sem=end_sem.at[1],
            device_id=(mate, core), device_id_type=MESH,
        )

    def swap(h):
        return pltpu.make_async_remote_copy(
            src_ref=map_hbm.at[h, pl.ds(0, 2)], dst_ref=mates.at[h], send_sem=mate_send.at[h], recv_sem=mate_recv.at[h],
            device_id=(mate, core), device_id_type=MESH,
        )

    def onward(h, i):
        return pltpu.make_async_remote_copy(
            src_ref=leaving.at[2 * h + i], dst_ref=arrived.at[2 * h + i],
            send_sem=send_sem.at[2 * h + i], recv_sem=recv_sem.at[2 * h + i],
            device_id=(after, core), device_id_type=MESH,
        )

    def sideways(h, i):
        return pltpu.make_async_remote_copy(
            src_ref=passing.at[2 * h + i], dst_ref=arrived.at[2 * h + i],
            send_sem=pass_sem.at[2 * h + i], recv_sem=recv_sem.at[2 * h + i],
            device_id=(mate, core), device_id_type=MESH,
        )

    def across(h):
        slot = gated.at[core * heads + h]
        return pltpu.make_async_remote_copy(
            src_ref=slot, dst_ref=slot, send_sem=gsend_sem.at[h], recv_sem=grecv_sem.at[h],
            device_id=(me, other), device_id_type=MESH,
        )

    barrier = pltpu.get_barrier_semaphore()
    pl.semaphore_signal(barrier, inc=1, device_id=(mate, core), device_id_type=MESH)
    pl.semaphore_signal(barrier, inc=1, device_id=(me, other), device_id_type=MESH)

    @pl.when(odd == 0)
    def _():
        pl.semaphore_signal(barrier, inc=1, device_id=(before, core), device_id_type=MESH)

    @pl.loop(0, heads)
    def _(h):
        load_map(h).start()
        load_add(h).start()

    @pl.when(me == 0)
    def _():
        arrived[...] = jnp.zeros_like(arrived)

    pl.semaphore_wait(barrier, 3 - odd)

    @pl.when(odd == 1)
    def _():
        swap_end().start()

        @pl.loop(0, heads)
        def _(h):
            swap(h).start()

    load = pltpu.make_async_copy(w_ref, w_vmem, w_sem)
    load.start()

    def ready(h):
        load_map(h).wait()
        load_add(h).wait()

        @pl.when(odd == 0)
        def _():
            swap(h).wait_recv()

    def join(h):
        mine, theirs = maps[h, 0], mates[h, 0]
        mine_end, theirs_end = end_ref[h], mate_end[h]
        add = adds[h, 0]
        joint_map[h] = (
            theirs_end * mine.astype(F32) + mine_end * theirs.astype(F32) + mm(theirs, mine)
        ).astype(BF16)
        joint_add[h] = theirs_end * add + mm_t(add.astype(BF16), theirs) + mates[h, 1].astype(F32)

    ready(0)

    @pl.when(odd == 0)
    def _():
        swap_end().wait_recv()
        join(0)

    @pl.loop(0, heads)
    def _(h):
        for i in range(2):

            @pl.when(me > 0)
            def _():
                onward(h, i).wait_recv()

            @pl.when(relays)
            def _():
                state = arrived[2 * h + i]
                moved = mm_t(state.astype(BF16), joint_map[h])
                end = end_ref[h] * mate_end[h]
                leaving[2 * h + i] = (end * state + joint_add[h, i * part : (i + 1) * part]) + moved
                onward(h, i).start()

        @pl.when(h < heads - 1)
        def _():
            ready(h + 1)

        @pl.when(odd == 0)
        def _():
            for i in range(2):
                state = arrived[2 * h + i]
                moved = mm_t(state.astype(BF16), maps[h, 0])
                passing[2 * h + i] = (end_ref[h] * state + adds[h, 0, i * part : (i + 1) * part]) + moved
                sideways(h, i).start()
            join(lax.rem(h + 1, heads))

        s_hi, s_lo = split(jnp.concatenate([arrived[2 * h], arrived[2 * h + 1]], axis=0))
        rows = mm_t(maps[h, 2], s_hi) + (mm_t(maps[h, 2], s_lo) + mm_t(maps[h, 3], s_hi)) + adds[h, 1]
        scale = lax.rsqrt(jnp.mean(rows * rows, axis=1, keepdims=True) + EPS)
        x = gate_ref[:, pl.ds(pl.multiple_of(h * DK, DK), DK)].astype(F32)
        gated[core * heads + h] = (rows * scale * gain_ref[...] * (x / (1.0 + jnp.exp(-x)))).astype(BF16)
        across(h).start()

    load.wait()

    def project(base):
        block = jnp.concatenate([gated[base + i] for i in range(group)], axis=1)
        start = pl.multiple_of(base * DK, group * DK)
        return mm(block, w_vmem[pl.ds(start, group * DK), :])

    total[...] = project(core * heads)

    @pl.loop(1, heads // group)
    def _(g):
        total[...] += project(core * heads + g * group)

    @pl.loop(0, heads // group)
    def _(g):
        for i in range(group):
            across(g * group + i).wait_recv()
        total[...] += project(other * heads + g * group)

    out_ref[...] = total[...].astype(out_ref.dtype)

    @pl.loop(0, heads)
    def _(h):
        across(h).wait_send()

        @pl.when(odd == 1)
        def _():
            swap(h).wait_send()

        @pl.when(odd == 0)
        def _():
            sideways(h, 0).wait_send()
            sideways(h, 1).wait_send()

        @pl.when(relays)
        def _():
            onward(h, 0).wait_send()
            onward(h, 1).wait_send()

    @pl.when(odd == 1)
    def _():
        swap_end().wait_send()


def shards(n, query, keys, values, beta, gate_log, house_count, out_gate, norm_gain, out_weight):
    tok = query.shape[0]
    heads = query.shape[1] // DK
    steps = NH * tok
    half = tok // 2
    width = out_weight.shape[1]
    active = (jnp.arange(NH, dtype=jnp.int32)[:, None] < house_count[None, :]).astype(F32)
    strength = (beta * active[:, None, :]).reshape(NH, heads, 2, half).transpose(1, 2, 0, 3).reshape(heads, steps)
    upper = (jnp.arange(tok)[:, None] <= jnp.arange(tok)[None, :]).astype(F32)
    cum = jnp.dot(gate_log, upper, precision=lax.Precision.HIGHEST)
    cum_steps = jnp.broadcast_to(cum.reshape(heads, 2, 1, half), (heads, 2, NH, half)).reshape(heads, steps)
    k2 = keys.reshape(2, half, NH, heads * DK).transpose(0, 2, 1, 3).reshape(steps, heads * DK)
    v2 = values.reshape(2, half, NH, heads * DK).transpose(0, 2, 1, 3).reshape(steps, heads * DK)
    ends = jnp.broadcast_to(jnp.exp(cum[:, tok - 1 :])[:, :, None], (heads, 1, DK))

    together = 4
    maps, adds = pl.pallas_call(
        functools.partial(prepare_kernel, together),
        grid=(heads // together,),
        in_specs=[
            pl.BlockSpec((steps, together * DK), lambda i: (0, i)),
            pl.BlockSpec((steps, together * DK), lambda i: (0, i)),
            pl.BlockSpec((tok, together * DK), lambda i: (0, i)),
            pl.BlockSpec((steps, heads), lambda i: (0, 0)),
            pl.BlockSpec((tok, heads), lambda i: (0, 0)),
            pl.BlockSpec((steps, heads), lambda i: (0, 0)),
            pl.BlockSpec((together, 1, steps), lambda i: (i, 0, 0)),
            pl.BlockSpec((together, 1, steps), lambda i: (i, 0, 0)),
        ],
        out_specs=[
            pl.BlockSpec((together, 4, tok, DK), lambda i: (i, 0, 0, 0)),
            pl.BlockSpec((together, 2, tok, DK), lambda i: (i, 0, 0, 0)),
        ],
        out_shape=[
            jax.ShapeDtypeStruct((heads, 4, tok, DK), BF16),
            jax.ShapeDtypeStruct((heads, 2, tok, DK), F32),
        ],
        compiler_params=pltpu.CompilerParams(vmem_limit_bytes=40 * MIB),
    )(k2, v2, query, cum_steps.T, cum.T, strength.T, cum_steps[:, None, :], strength[:, None, :])

    group = 4
    vmem = pl.BlockSpec(memory_space=pltpu.VMEM)
    hbm = pl.BlockSpec(memory_space=pltpu.HBM)
    return pl.pallas_call(
        functools.partial(relay_kernel, n, heads, group),
        in_specs=[hbm, hbm, vmem, vmem, vmem, hbm],
        out_specs=vmem,
        out_shape=jax.ShapeDtypeStruct((tok, width), BF16),
        scratch_shapes=[
            pltpu.VMEM(out_weight.shape, BF16),
            pltpu.VMEM((heads, 4, tok, DK), BF16),
            pltpu.VMEM((heads, 2, tok, DK), F32),
            pltpu.VMEM((heads, 2, DK, DK), BF16),
            pltpu.VMEM(ends.shape, F32),
            pltpu.VMEM((heads, DK, DK), BF16),
            pltpu.VMEM((heads, DK, DK), F32),
            pltpu.VMEM((2 * heads, DK // 2, DK), F32),
            pltpu.VMEM((2 * heads, DK // 2, DK), F32),
            pltpu.VMEM((2 * heads, DK // 2, DK), F32),
            pltpu.VMEM((2 * heads, tok, DK), BF16),
            pltpu.VMEM((tok, width), F32),
            pltpu.SemaphoreType.DMA,
            pltpu.SemaphoreType.DMA((heads,)),
            pltpu.SemaphoreType.DMA((heads,)),
            pltpu.SemaphoreType.DMA((2,)),
            pltpu.SemaphoreType.DMA((heads,)),
            pltpu.SemaphoreType.DMA((heads,)),
            pltpu.SemaphoreType.DMA((2 * heads,)),
            pltpu.SemaphoreType.DMA((2 * heads,)),
            pltpu.SemaphoreType.DMA((2 * heads,)),
            pltpu.SemaphoreType.DMA((heads,)),
            pltpu.SemaphoreType.DMA((heads,)),
        ],
        compiler_params=pltpu.CompilerParams(
            collective_id=0, has_side_effects=True, vmem_limit_bytes=56 * MIB
        ),
    )(maps, adds, out_gate, ends, norm_gain[None, :], out_weight)


def solution(mesh):
    return jax.shard_map(
        functools.partial(shards, mesh.shape["seq"]),
        mesh=mesh,
        in_specs=(
            P("seq", "head"),
            P("seq", None, "head"),
            P("seq", None, "head"),
            P(None, "head", "seq"),
            P("head", "seq"),
            P("seq"),
            P("seq", "head"),
            P(),
            P(None, "head"),
        ),
        out_specs=P("seq", "head"),
        check_vma=False,
    )
```

```python
import functools

import jax
import jax.numpy as jnp
from jax import lax
from jax.experimental import pallas as pl
from jax.experimental.pallas import tpu as pltpu
from jax.sharding import PartitionSpec as P

DK = 128
NH = 2
EPS = 1e-06
F32 = jnp.float32
BF16 = jnp.bfloat16
MESH = pl.DeviceIdType.MESH
MIB = 1024 * 1024


def mm(a, b):
    return jnp.dot(a, b, preferred_element_type=F32)


def mm_t(a, b):
    return lax.dot_general(a, b, (((1,), (1,)), ((), ())), preferred_element_type=F32)


def t_mm(a, b):
    return lax.dot_general(a, b, (((0,), (0,)), ((), ())), preferred_element_type=F32)


def split(x):
    hi = x.astype(BF16)
    return hi, (x - hi.astype(F32)).astype(BF16)


def mm3(a, b):
    return mm(a[0], b[0]) + (mm(a[0], b[1]) + mm(a[1], b[0]))


def prepare(group):
    tok = group[0]["q"].shape[0]
    span = tok
    half = tok // 2
    row_at = lax.broadcasted_iota(jnp.int32, (span, span), 0)
    col_at = lax.broadcasted_iota(jnp.int32, (span, span), 1)

    def time_of(index):
        return jnp.where(index < half, 2 * index, 2 * (index - half) + 1)

    row_time, col_time = time_of(row_at), time_of(col_at)
    apart = row_time ^ col_time
    strictly = row_time > col_time
    diagonal = row_at == col_at
    unit = jnp.where(diagonal, 1.0, 0.0)
    token_at = jnp.where(col_at < half, col_at, col_at - half)
    seen = [row_at >= token_at, row_at >= token_at + half]
    blocks = [slice(0, span), slice(span, 2 * span)]

    lowers, corners, norms = [], [], []
    for x in group:
        k = [x["k"][b] for b in blocks]
        grams = [mm_t(kb, kb) for kb in k]
        cross = mm_t(k[1], k[0])
        on_diag = [jnp.where(diagonal, g, 0.0) for g in grams]
        rk_row = [lax.rsqrt(jnp.sum(d, axis=0, keepdims=True) + EPS) for d in on_diag]
        rk_col = [lax.rsqrt(jnp.sum(d, axis=1, keepdims=True) + EPS) for d in on_diag]
        cr = [x["cum_row"][:, b] for b in blocks]
        cc = [x["cum_col"][b] for b in blocks]
        sc = [x["s_col"][b] for b in blocks]
        for b in range(2):
            fade = jnp.exp(jnp.where(strictly, cc[b] - cr[b], 0.0))
            lowers.append(jnp.where(strictly, (sc[b] * rk_col[b]) * (grams[b] * fade) * rk_row[b], 0.0))
        corners.append((sc[1] * rk_col[1]) * (cross * jnp.exp(cc[1] - cr[0])) * rk_row[0])
        norms.append((rk_row, rk_col, cr, cc, sc))

    inverses = [unit - jnp.where(apart == 1, low, 0.0) for low in lowers]
    width = 2
    while width < span:
        here = (apart >= width) & (apart < 2 * width)
        rounded = [inv.astype(BF16) for inv in inverses]
        firsts = [mm(r, jnp.where(here, low, 0.0).astype(BF16)).astype(BF16) for r, low in zip(rounded, lowers)]
        inverses = [inv - mm(f, r) for inv, f, r in zip(inverses, firsts, rounded)]
        width *= 2
    parts = [split(inv) for inv in inverses]
    residuals = [unit - inv - mm3(split(low), p) for inv, low, p in zip(inverses, lowers, parts)]
    inverses = [inv + mm(p[0], r.astype(BF16)) for inv, p, r in zip(inverses, parts, residuals)]

    firsts = []
    for i, x in enumerate(group):
        rk_row, _, cr, _, _ = norms[i]
        by_value = inverses[2 * i] * x["s_row"][:, blocks[0]]
        val_hi, val_lo = split(by_value)
        key_hi, key_lo = split(by_value * (jnp.exp(cr[0]) * rk_row[0]))
        k, v = x["k"][blocks[0]], x["v"][blocks[0]]
        firsts.append(jnp.concatenate([mm(key_hi, k) + mm(key_lo, k), mm(val_hi, v) + mm(val_lo, v)], axis=1))
    first_parts = [split(f) for f in firsts]
    seconds = []
    for i, x in enumerate(group):
        _, rk_col, _, cc, sc = norms[i]
        k, v = x["k"][blocks[1]].astype(F32), x["v"][blocks[1]].astype(F32)
        right = jnp.concatenate([(sc[1] * jnp.exp(cc[1]) * rk_col[1]) * k, sc[1] * v], axis=1)
        right = right - mm3(split(corners[i]), first_parts[i])
        seconds.append(mm3(split(inverses[2 * i + 1]), split(right)))
    second_parts = [split(s) for s in seconds]

    results = []
    for i, x in enumerate(group):
        rk_row, rk_col, cr, cc, _ = norms[i]
        end = x["cum_row"][:, 2 * span - 1 :]
        ctok = x["cum_tok"]
        q = x["q"]
        qf = q.astype(F32)
        rq = lax.rsqrt(jnp.sum(qf * qf, axis=1, keepdims=True) + EPS)
        mult, add, read = 0.0, 0.0, 0.0
        for b, (whole, pieces) in enumerate([(firsts[i], first_parts[i]), (seconds[i], second_parts[i])]):
            kb = x["k"][blocks[b]]
            faded_hi, faded_lo = split((jnp.exp(end - cc[b]) * rk_col[b]) * whole)
            mult = mult - t_mm(kb, faded_hi[:, :DK])
            add = add + (t_mm(faded_hi[:, DK:], kb) + t_mm(faded_lo[:, DK:], kb))
            lag = jnp.exp(jnp.where(seen[b], ctok - cr[b], 0.0))
            weights = jnp.where(seen[b], (rq * rk_row[b]) * (lag * mm_t(q, kb)), 0.0)
            read = read + mm3(split(weights), pieces)
        query_hi, query_lo = split((jnp.exp(ctok) * rq) * qf - read[:, :DK])
        results.append((mult.astype(BF16), add.astype(BF16), query_hi, query_lo, add, read[:, DK:]))
    return results


def prepare_kernel(together, k_ref, v_ref, q_ref, cumt_ref, ctok_ref, st_ref, cum_ref, s_ref, map_ref, add_ref):
    def column(ref, head):
        lane = lax.broadcasted_iota(jnp.int32, ref.shape, 1)
        return jnp.sum(jnp.where(lane == head, ref[...], 0.0), axis=1, keepdims=True)

    group = []
    for i in range(together):
        head = pl.program_id(0) * together + i
        cols = slice(i * DK, (i + 1) * DK)
        group.append(dict(
            k=k_ref[:, cols], v=v_ref[:, cols], q=q_ref[:, cols],
            cum_col=column(cumt_ref, head), cum_tok=column(ctok_ref, head), s_col=column(st_ref, head),
            cum_row=cum_ref[i], s_row=s_ref[i],
        ))
    for i, (mult, add_low, query_hi, query_lo, add, local) in enumerate(prepare(group)):
        map_ref[i, 0], map_ref[i, 1] = mult, add_low
        map_ref[i, 2], map_ref[i, 3] = query_hi, query_lo
        add_ref[i, 0], add_ref[i, 1] = add, local


def relay_kernel(
    n, heads, group, map_hbm, add_hbm, gate_ref, end_ref, gain_ref, w_ref, out_ref,
    w_vmem, maps, adds, mates, mate_end, joint_map, joint_add, arrived, leaving, passing, gated, total,
    w_sem, map_sem, add_sem, end_sem, mate_send, mate_recv, send_sem, pass_sem, recv_sem, gsend_sem, grecv_sem,
):
    me = lax.axis_index("seq")
    core = lax.axis_index("head")
    odd = lax.rem(me, 2)
    first = me - odd
    mate = me + 1 - 2 * odd
    after, before = lax.rem(first + 2, n), lax.rem(first + n - 2, n)
    other = 1 - core
    part = DK // 2
    relays = (odd == 0) & (me < n - 2)
    late = me >= n // 2

    def load_map(h):
        return pltpu.make_async_copy(map_hbm.at[h], maps.at[h], map_sem.at[h])

    def load_add(h):
        return pltpu.make_async_copy(add_hbm.at[h], adds.at[h], add_sem.at[h])

    def swap_end():
        return pltpu.make_async_remote_copy(
            src_ref=end_ref, dst_ref=mate_end, send_sem=end_sem.at[0], recv_sem=end_sem.at[1],
            device_id=(mate, core), device_id_type=MESH,
        )

    def swap(h):
        return pltpu.make_async_remote_copy(
            src_ref=map_hbm.at[h, pl.ds(0, 2)], dst_ref=mates.at[h], send_sem=mate_send.at[h], recv_sem=mate_recv.at[h],
            device_id=(mate, core), device_id_type=MESH,
        )

    def onward(h, i):
        return pltpu.make_async_remote_copy(
            src_ref=leaving.at[2 * h + i], dst_ref=arrived.at[2 * h + i],
            send_sem=send_sem.at[2 * h + i], recv_sem=recv_sem.at[2 * h + i],
            device_id=(after, core), device_id_type=MESH,
        )

    def sideways(h, i):
        return pltpu.make_async_remote_copy(
            src_ref=passing.at[2 * h + i], dst_ref=arrived.at[2 * h + i],
            send_sem=pass_sem.at[2 * h + i], recv_sem=recv_sem.at[2 * h + i],
            device_id=(mate, core), device_id_type=MESH,
        )

    def across(h):
        slot = gated.at[core * heads + h]
        return pltpu.make_async_remote_copy(
            src_ref=slot, dst_ref=slot, send_sem=gsend_sem.at[h], recv_sem=grecv_sem.at[h],
            device_id=(me, other), device_id_type=MESH,
        )

    barrier = pltpu.get_barrier_semaphore()
    pl.semaphore_signal(barrier, inc=1, device_id=(mate, core), device_id_type=MESH)
    pl.semaphore_signal(barrier, inc=1, device_id=(me, other), device_id_type=MESH)

    @pl.when(odd == 0)
    def _():
        pl.semaphore_signal(barrier, inc=1, device_id=(before, core), device_id_type=MESH)

    @pl.loop(0, heads)
    def _(h):
        load_map(h).start()
        load_add(h).start()

    @pl.when(me == 0)
    def _():
        arrived[...] = jnp.zeros_like(arrived)

    pl.semaphore_wait(barrier, 3 - odd)

    @pl.when(odd == 1)
    def _():
        swap_end().start()

        @pl.loop(0, heads)
        def _(h):
            swap(h).start()

    load = pltpu.make_async_copy(w_ref, w_vmem, w_sem)
    load.start()

    def ready(h):
        load_map(h).wait()
        load_add(h).wait()

        @pl.when(odd == 0)
        def _():
            swap(h).wait_recv()

    def join(h):
        mine, theirs = maps[h, 0], mates[h, 0]
        mine_end, theirs_end = end_ref[h], mate_end[h]
        add = adds[h, 0]
        joint_map[h] = (
            theirs_end * mine.astype(F32) + mine_end * theirs.astype(F32) + mm(theirs, mine)
        ).astype(BF16)
        joint_add[h] = theirs_end * add + mm_t(add.astype(BF16), theirs) + mates[h, 1].astype(F32)

    def project(base):
        block = jnp.concatenate([gated[base + i] for i in range(group)], axis=1)
        start = pl.multiple_of(base * DK, group * DK)
        return mm(block, w_vmem[pl.ds(start, group * DK), :])

    total[...] = jnp.zeros_like(total)

    @pl.when(late)
    def _():
        load.wait()

    ready(0)

    @pl.when(odd == 0)
    def _():
        swap_end().wait_recv()
        join(0)

    @pl.loop(0, heads)
    def _(h):
        for i in range(2):

            @pl.when(me > 0)
            def _():
                onward(h, i).wait_recv()

            @pl.when(relays)
            def _():
                state = arrived[2 * h + i]
                moved = mm_t(state.astype(BF16), joint_map[h])
                end = end_ref[h] * mate_end[h]
                leaving[2 * h + i] = (end * state + joint_add[h, i * part : (i + 1) * part]) + moved
                onward(h, i).start()

        @pl.when(h < heads - 1)
        def _():
            ready(h + 1)

        @pl.when(odd == 0)
        def _():
            for i in range(2):
                state = arrived[2 * h + i]
                moved = mm_t(state.astype(BF16), maps[h, 0])
                passing[2 * h + i] = (end_ref[h] * state + adds[h, 0, i * part : (i + 1) * part]) + moved
                sideways(h, i).start()
            join(lax.rem(h + 1, heads))

        s_hi, s_lo = split(jnp.concatenate([arrived[2 * h], arrived[2 * h + 1]], axis=0))
        rows = mm_t(maps[h, 2], s_hi) + (mm_t(maps[h, 2], s_lo) + mm_t(maps[h, 3], s_hi)) + adds[h, 1]
        scale = lax.rsqrt(jnp.mean(rows * rows, axis=1, keepdims=True) + EPS)
        x = gate_ref[:, pl.ds(pl.multiple_of(h * DK, DK), DK)].astype(F32)
        gated[core * heads + h] = (rows * scale * gain_ref[...] * (x / (1.0 + jnp.exp(-x)))).astype(BF16)
        across(h).start()

        @pl.when(late & (lax.rem(h, group) == group - 1))
        def _():
            total[...] += project(core * heads + (h - (group - 1)))

    @pl.when(jnp.logical_not(late))
    def _():
        load.wait()

        @pl.loop(0, heads // group)
        def _(g):
            total[...] += project(core * heads + g * group)

    @pl.loop(0, heads // group)
    def _(g):
        for i in range(group):
            across(g * group + i).wait_recv()
        total[...] += project(other * heads + g * group)

    out_ref[...] = total[...].astype(out_ref.dtype)

    @pl.loop(0, heads)
    def _(h):
        across(h).wait_send()

        @pl.when(odd == 1)
        def _():
            swap(h).wait_send()

        @pl.when(odd == 0)
        def _():
            sideways(h, 0).wait_send()
            sideways(h, 1).wait_send()

        @pl.when(relays)
        def _():
            onward(h, 0).wait_send()
            onward(h, 1).wait_send()

    @pl.when(odd == 1)
    def _():
        swap_end().wait_send()


def shards(n, query, keys, values, beta, gate_log, house_count, out_gate, norm_gain, out_weight):
    tok = query.shape[0]
    heads = query.shape[1] // DK
    steps = NH * tok
    half = tok // 2
    width = out_weight.shape[1]
    active = (jnp.arange(NH, dtype=jnp.int32)[:, None] < house_count[None, :]).astype(F32)
    strength = (beta * active[:, None, :]).reshape(NH, heads, 2, half).transpose(1, 2, 0, 3).reshape(heads, steps)
    upper = (jnp.arange(tok)[:, None] <= jnp.arange(tok)[None, :]).astype(F32)
    cum = jnp.dot(gate_log, upper, precision=lax.Precision.HIGHEST)
    cum_steps = jnp.broadcast_to(cum.reshape(heads, 2, 1, half), (heads, 2, NH, half)).reshape(heads, steps)
    k2 = keys.reshape(2, half, NH, heads * DK).transpose(0, 2, 1, 3).reshape(steps, heads * DK)
    v2 = values.reshape(2, half, NH, heads * DK).transpose(0, 2, 1, 3).reshape(steps, heads * DK)
    ends = jnp.broadcast_to(jnp.exp(cum[:, tok - 1 :])[:, :, None], (heads, 1, DK))

    together = 4
    maps, adds = pl.pallas_call(
        functools.partial(prepare_kernel, together),
        grid=(heads // together,),
        in_specs=[
            pl.BlockSpec((steps, together * DK), lambda i: (0, i)),
            pl.BlockSpec((steps, together * DK), lambda i: (0, i)),
            pl.BlockSpec((tok, together * DK), lambda i: (0, i)),
            pl.BlockSpec((steps, heads), lambda i: (0, 0)),
            pl.BlockSpec((tok, heads), lambda i: (0, 0)),
            pl.BlockSpec((steps, heads), lambda i: (0, 0)),
            pl.BlockSpec((together, 1, steps), lambda i: (i, 0, 0)),
            pl.BlockSpec((together, 1, steps), lambda i: (i, 0, 0)),
        ],
        out_specs=[
            pl.BlockSpec((together, 4, tok, DK), lambda i: (i, 0, 0, 0)),
            pl.BlockSpec((together, 2, tok, DK), lambda i: (i, 0, 0, 0)),
        ],
        out_shape=[
            jax.ShapeDtypeStruct((heads, 4, tok, DK), BF16),
            jax.ShapeDtypeStruct((heads, 2, tok, DK), F32),
        ],
        compiler_params=pltpu.CompilerParams(vmem_limit_bytes=40 * MIB),
    )(k2, v2, query, cum_steps.T, cum.T, strength.T, cum_steps[:, None, :], strength[:, None, :])

    group = 4
    vmem = pl.BlockSpec(memory_space=pltpu.VMEM)
    hbm = pl.BlockSpec(memory_space=pltpu.HBM)
    return pl.pallas_call(
        functools.partial(relay_kernel, n, heads, group),
        in_specs=[hbm, hbm, vmem, vmem, vmem, hbm],
        out_specs=vmem,
        out_shape=jax.ShapeDtypeStruct((tok, width), BF16),
        scratch_shapes=[
            pltpu.VMEM(out_weight.shape, BF16),
            pltpu.VMEM((heads, 4, tok, DK), BF16),
            pltpu.VMEM((heads, 2, tok, DK), F32),
            pltpu.VMEM((heads, 2, DK, DK), BF16),
            pltpu.VMEM(ends.shape, F32),
            pltpu.VMEM((heads, DK, DK), BF16),
            pltpu.VMEM((heads, DK, DK), F32),
            pltpu.VMEM((2 * heads, DK // 2, DK), F32),
            pltpu.VMEM((2 * heads, DK // 2, DK), F32),
            pltpu.VMEM((2 * heads, DK // 2, DK), F32),
            pltpu.VMEM((2 * heads, tok, DK), BF16),
            pltpu.VMEM((tok, width), F32),
            pltpu.SemaphoreType.DMA,
            pltpu.SemaphoreType.DMA((heads,)),
            pltpu.SemaphoreType.DMA((heads,)),
            pltpu.SemaphoreType.DMA((2,)),
            pltpu.SemaphoreType.DMA((heads,)),
            pltpu.SemaphoreType.DMA((heads,)),
            pltpu.SemaphoreType.DMA((2 * heads,)),
            pltpu.SemaphoreType.DMA((2 * heads,)),
            pltpu.SemaphoreType.DMA((2 * heads,)),
            pltpu.SemaphoreType.DMA((heads,)),
            pltpu.SemaphoreType.DMA((heads,)),
        ],
        compiler_params=pltpu.CompilerParams(
            collective_id=0, has_side_effects=True, vmem_limit_bytes=56 * MIB
        ),
    )(maps, adds, out_gate, ends, norm_gain[None, :], out_weight)


def solution(mesh):
    return jax.shard_map(
        functools.partial(shards, mesh.shape["seq"]),
        mesh=mesh,
        in_specs=(
            P("seq", "head"),
            P("seq", None, "head"),
            P("seq", None, "head"),
            P(None, "head", "seq"),
            P("head", "seq"),
            P("seq"),
            P("seq", "head"),
            P(),
            P(None, "head"),
        ),
        out_specs=P("seq", "head"),
        check_vma=False,
    )
```
